128 devices in a mesh: blk: 64 (over z_lo, x, y, core), head: 2 (over z_hi).
Axes of the slice: x: 4, y: 4, z: 4 (z_hi: 2, z_lo: 2; z = z_hi * 2 + z_lo), core: 2. Of those that a mesh axis runs over, the one named last changes fastest.
Arguments:
- prefix: bfloat16 [24576, 2048], P(('blk', 'head')), may hold values from -30 to 30
- w_key: bfloat16 [2048, 2048], P(None, 'head'), may hold values from -1 to 1.5
- w_value: bfloat16 [2048, 2048], P(None, 'head'), may hold values from -0.125 to 0.125
- queries: bfloat16 [2048, 2048], P('blk', 'head'), may hold values from -100 to 100
- output_grad: bfloat16 [2048, 2048], P('blk', 'head'), may hold values from -6 to 6
- block_mask: int32 [64, 192], P(None, 'blk'), may hold values from 0 to 1, as said below
Outputs:
- query_grads: bfloat16 [2048, 2048], P('blk', 'head')
- prefix_grads: bfloat16 [24576, 2048], P(('blk', 'head'))
The draws below stay inside these ranges and needn't reach their ends.
Inputs may be any that keep to these rules, and one draw needn't show every extreme that they name: block_mask[j, c] is 1 where latents j * 32 to (j + 1) * 32 - 1 attend to prefix tokens c * 128 to (c + 1) * 128 - 1, else 0; block_mask[j, j * 3] is 1 for every j.
All inputs are finite; a program needn't handle non-finite values.
Results may differ from the reference program's by a relative error of at most 0.0095.
The reference program's roundings to bfloat16 on the way (of `key_rows`, `value_rows`, `attention_low`, `lowered_grad`, `key_grads` and `value_grads`) count: a program that leaves them out, or rounds other values in their place, can miss the bound.
Values may be sent and summed in bfloat16 or wider, within the bound.
A program may use at most 128 MiB of HBM per device.

```python
import math
import jax
import jax.numpy as jnp
from jax import lax

D = 2048
HEADS = 16
HEAD_DIM = 128
BLOCK = 128
LAT_DEV = 32
SHARDS = 64
LATENTS = 2048
PREFIX = 24576
PB = 3
NBLOCKS = 192


def draw_queries(key, part):
    key = jax.random.fold_in(key, 11)
    base = jnp.clip(jax.random.normal(jax.random.fold_in(key, 1), (LATENTS, D), jnp.float32), -6.0, 6.0)
    return base.astype(jnp.bfloat16)


def draw_prefix(key, part):
    key = jax.random.fold_in(key, 13)
    base = jnp.clip(jax.random.normal(jax.random.fold_in(key, 1), (PREFIX, D), jnp.float32), -6.0, 6.0)
    return base.astype(jnp.bfloat16)


def draw_w_key(key, part):
    key = jax.random.fold_in(key, 17)
    noise = jnp.clip(jax.random.normal(jax.random.fold_in(key, 1), (D, D), jnp.float32), -6.0, 6.0) / math.sqrt(D)
    return noise.astype(jnp.bfloat16)


def draw_block_mask(key, part):
    key = jax.random.fold_in(key, 19)
    density = jax.random.randint(jax.random.fold_in(key, 1), (SHARDS,), 10, 80)
    columns = jnp.arange(NBLOCKS, dtype=jnp.int32)
    device_ids = columns // PB
    rolls = jax.random.randint(jax.random.fold_in(key, 2), (SHARDS, NBLOCKS), 0, 100)
    chosen = rolls < density[device_ids][None, :]
    own_block = columns[None, :] == jnp.arange(SHARDS, dtype=jnp.int32)[:, None] * PB
    return jnp.where(chosen | own_block, 1, 0).astype(jnp.int32)


def block_levels(own_key, dims, pieces, low, largest):
    factor_of, own = 1.0, jax.random.fold_in(own_key, 6)
    for dim, parts in pieces:
        draws = jnp.exp(jax.random.uniform(jax.random.fold_in(own, dim), (parts,), jnp.float32, low / len(pieces), largest / len(pieces)))
        factor_of = factor_of * jnp.repeat(draws, dims[dim] // parts).reshape([-1 if axis == dim else 1 for axis in range(len(dims))])
    return factor_of


def normal_values(stream_key, shape, deviation, reach, shards=(), held_as=jnp.bfloat16):
    values = jax.random.normal(stream_key, shape, jnp.float32) * deviation
    if len(shards) > 0:
        values = block_levels(stream_key, shape, shards, -0.22, 0.18) * values
    return jnp.clip(values, min=-reach, max=reach).astype(held_as)


def setup_inputs(seed: int = 0) -> dict:
    streams_of = jax.random.split(jax.random.key(seed), 7)
    return {
        "prefix": draw_prefix(jax.random.fold_in(streams_of[6], 71), 0),
        "w_key": draw_w_key(jax.random.fold_in(streams_of[6], 71), 0),
        "w_value": normal_values(streams_of[2], (D, D), D ** -0.5, 0.125, ((1, 2),)),
        "queries": draw_queries(jax.random.fold_in(streams_of[6], 71), 0),
        "output_grad": normal_values(streams_of[4], (LATENTS, D), 1.0, 6.0, ((0, 64), (1, 2))),
        "block_mask": draw_block_mask(jax.random.fold_in(streams_of[6], 71), 0),
    }


NEG_FILL = -1e+30

def split_heads(matrix):
    height = matrix.shape[0]
    return matrix.astype(jnp.float32).reshape(height, HEADS, HEAD_DIM).transpose(1, 0, 2)

def join_heads(stacked):
    return stacked.transpose(1, 0, 2).reshape(stacked.shape[1], HEADS * HEAD_DIM)

def reference(prefix, w_key, w_value, queries, output_grad, block_mask):
    score_scale = 1.0 / math.sqrt(HEAD_DIM)
    exact_mode = lax.Precision.HIGHEST
    key_rows = lax.optimization_barrier(jnp.dot(prefix, w_key, preferred_element_type=jnp.float32).astype(jnp.bfloat16))
    value_rows = lax.optimization_barrier(jnp.dot(prefix, w_value, preferred_element_type=jnp.float32).astype(jnp.bfloat16))
    live_cells = jnp.repeat(jnp.repeat(block_mask != 0, LAT_DEV, axis=0), BLOCK, axis=1)

    def one_head(operands):
        query_head, key_head, value_head, grad_head = operands
        scores = jnp.dot(query_head, key_head.T, precision=exact_mode, preferred_element_type=jnp.float32) * score_scale
        scores = jnp.where(live_cells, scores, NEG_FILL)
        row_top = lax.optimization_barrier(jnp.max(scores, axis=1, keepdims=True))
        row_total = lax.optimization_barrier(jnp.sum(jnp.where(live_cells, jnp.exp(scores - row_top), 0.0), axis=1, keepdims=True))
        log_total = row_top + jnp.log(row_total)
        attention = jnp.where(live_cells, jnp.exp(scores - log_total), 0.0)
        output_dots = jnp.dot(grad_head, value_head.T, precision=exact_mode, preferred_element_type=jnp.float32)
        row_delta = lax.optimization_barrier(jnp.sum(attention * output_dots, axis=1, keepdims=True))
        score_grad = attention * (output_dots - row_delta)
        attention_low = lax.optimization_barrier(attention.astype(jnp.bfloat16)).astype(jnp.float32)
        lowered_grad = lax.optimization_barrier(score_grad.astype(jnp.bfloat16)).astype(jnp.float32)
        query_grad = jnp.dot(lowered_grad, key_head, precision=exact_mode, preferred_element_type=jnp.float32) * score_scale
        key_grad = jnp.einsum('ip,id->pd', lowered_grad, query_head, precision=exact_mode) * score_scale
        value_grad = jnp.einsum('ip,id->pd', attention_low, grad_head, precision=exact_mode)
        return (query_grad, key_grad.astype(jnp.bfloat16), value_grad.astype(jnp.bfloat16))
    query_grad, key_grad, value_grad = lax.map(one_head, (split_heads(queries), split_heads(key_rows), split_heads(value_rows), split_heads(output_grad)))
    query_grads = join_heads(query_grad).astype(jnp.bfloat16)
    key_grads = join_heads(key_grad)
    value_grads = join_heads(value_grad)
    prefix_grads = jnp.dot(key_grads, w_key.T, preferred_element_type=jnp.float32) + jnp.dot(value_grads, w_value.T, preferred_element_type=jnp.float32)
    return (query_grads, prefix_grads.astype(jnp.bfloat16))
```

```python
import math

import jax
import jax.numpy as jnp
from jax import lax
from jax.experimental import pallas as pl
from jax.experimental.pallas import tpu as pltpu
from jax.sharding import PartitionSpec as P

MESH = pl.DeviceIdType.MESH
HEAD_DIM = 128
BLOCK = 128
UNIT = 64
FILL = -1e30
F32 = jnp.float32
BF16 = jnp.bfloat16

NZ, NX, NY = 2, 4, 4
PEERS = NZ * NX * NY
HEADS = 8
LAT = 32
ROWS = 192
COLS = HEADS * HEAD_DIM
D = 2048
LATENTS = PEERS * LAT
TILE = 256
TILES = LATENTS // TILE
STEPS = HEADS * TILES
LAG = 4
CHUNKS = 2
GROUPS = 4
SCALE = 1.0 / math.sqrt(HEAD_DIM)
SCALE2 = SCALE * math.log2(math.e)
NT = (((1,), (1,)), ((), ()))
TN = (((0,), (0,)), ((), ()))
NN = (((1,), (0,)), ((), ()))


def dot(a, b, dims):
    return lax.dot_general(a, b, dims, preferred_element_type=F32)


def lanes(index, width):
    return pl.ds(pl.multiple_of(index * width, width), width)


def kernel(
    prefix, w_key, w_value, queries, grads, mask,
    dq_out, pg_out,
    w, pref, gat, kv, mask_in, bias, stat, stat_in, glob, p_low, s_low, dq, r1, r2, r3, r4, r5,
    dkv, dkv_in, low, back, back_in,
    w_sem, own_sem, send_sem, recv_sem, stat_send, stat_recv, glob_send, glob_recv,
    dkv_send, dkv_recv, back_send, back_recv,
):
    b = lax.axis_index("blk")
    head = lax.axis_index("head")
    core = lax.rem(b, 2)
    me = lax.div(b, 2)
    y = lax.rem(me, NY)
    x = lax.rem(lax.div(me, NY), NX)
    z = lax.div(me, NX * NY)

    def peer(index):
        return (2 * index + core, head)

    def at(z_, x_, y_):
        return peer((z_ * NX + x_) * NY + y_)

    up = lambda v, k: lax.rem(v + k, 4)
    x1, x2, x3 = up(x, 1), up(x, 2), up(x, 3)
    y1, y2, y3 = up(y, 1), up(y, 2), up(y, 3)
    xp, xm, yp, ym, zn = at(z, x1, y), at(z, x3, y), at(z, x, y1), at(z, x, y3), at(1 - z, x, y)
    sibling = (2 * me + 1 - core, head)
    partner = (b, 1 - head)

    barrier = pltpu.get_barrier_semaphore()

    def greet(k, carry):
        pl.semaphore_signal(
            barrier, inc=1, device_id=peer(lax.rem(me + k, PEERS)), device_id_type=MESH
        )
        return carry

    lax.fori_loop(1, PEERS, greet, 0)
    pl.semaphore_signal(barrier, inc=1, device_id=sibling, device_id_type=MESH)
    pl.semaphore_signal(barrier, inc=1, device_id=partner, device_id_type=MESH)

    w_copies = [
        pltpu.make_async_copy(w_key, w.at[0], w_sem.at[0]),
        pltpu.make_async_copy(w_value, w.at[1], w_sem.at[1]),
    ]
    for copy in w_copies:
        copy.start()
    pl.semaphore_wait(barrier, PEERS + 1)

    used = []

    def send(src, dst, device):
        index = len(used)
        copy = pltpu.make_async_remote_copy(
            src_ref=src, dst_ref=dst, send_sem=send_sem.at[index], recv_sem=recv_sem.at[index],
            device_id=device, device_id_type=MESH,
        )
        copy.start()
        used.append(copy)
        return copy

    shards = (queries, grads)
    rings = (((xp, xm, x, x1, x3), (yp, ym, y, y1, y3)), ((yp, ym, y, y1, y3), (xp, xm, x, x1, x3)))

    def block(t, z_, first, second, cols):
        if t == 0:
            return gat.at[0, z_, first, second, :, cols]
        return gat.at[1, z_, second, first, :, cols]

    def line(t, z_, second, cols):
        if t == 0:
            return gat.at[0, z_, :, second, :, cols]
        return gat.at[1, z_, second, :, :, cols]

    width = COLS // CHUNKS
    flight = {}

    def relay(c, step):
        cols = pl.ds(c * width, width)
        for t in range(2):
            (p1, m1, a, a_up, a_dn), (p2, m2, e, e_up, e_dn) = rings[t]
            key = (c, t)
            if step == 0:
                mine = shards[t].at[:, cols]
                dst = block(t, z, a, e, cols)
                own = pltpu.make_async_copy(mine, dst, own_sem.at[2 * c + t])
                own.start()
                flight[key] = [send(mine, dst, zn), send(mine, dst, p1), send(mine, dst, m1), own]
            elif step == 1:
                flight[key][0].wait_recv()
                src = block(t, 1 - z, a, e, cols)
                flight[key] += [send(src, src, p1), send(src, src, m1)]
            elif step == 2:
                for k in (1, 2, 4, 5):
                    flight[key][k].wait_recv()
                flight[key][3].wait()
                lo, hi = block(t, 0, a_dn, e, cols), block(t, 1, a_up, e, cols)
                flight[key] = [send(lo, lo, p1), send(hi, hi, m1)]
            elif step == 3:
                for k in (0, 1):
                    flight[key][k].wait_recv()
                flight[key] = []
                for z_ in range(NZ):
                    src = line(t, z_, e, cols)
                    flight[key] += [send(src, src, p2), send(src, src, m2)]
            elif step == 4:
                for k in range(4):
                    flight[key][k].wait_recv()
                lo, hi = line(t, 0, e_dn, cols), line(t, 1, e_up, cols)
                flight[key] = [send(lo, lo, p2), send(hi, hi, m2)]
            else:
                for k in (0, 1):
                    flight[key][k].wait_recv()

    for c in range(CHUNKS):
        relay(c, 0)
    pref_copy = send(prefix, pref, partner)
    mask_copy = send(mask.at[1 - core], mask_in, sibling)

    def project(rows, half):
        def column(j, carry):
            for i in range(2):
                cols = lanes(j, 256)
                kv[i, core, half, :, cols] = dot(rows[...], w[i, :, cols], NN).astype(BF16)
            return carry

        lax.fori_loop(0, COLS // 256, column, 0)
        return [send(kv.at[i, core, half], kv.at[i, core, half], sibling) for i in range(2)]

    relay(0, 1)
    relay(1, 1)
    for copy in w_copies:
        copy.wait()
    kv_copies = project(prefix, head)
    relay(0, 2)
    relay(1, 2)

    which = lax.broadcasted_iota(jnp.int32, (BLOCK, LATENTS), 0)
    latent = lax.broadcasted_iota(jnp.int32, (BLOCK, LATENTS), 1)
    spread = jnp.where(lax.div(latent, LAT) == which, 1.0, 0.0).astype(BF16)

    def fill_bias(row_core, source):
        for half in range(2):
            live = dot(source[half].astype(BF16), spread, NN)
            bias[row_core, half] = jnp.where(live > 0.5, 0.0, FILL)

    fill_bias(core, mask[core])
    mask_copy.wait_recv()
    fill_bias(1 - core, mask_in[...])
    relay(0, 3)
    relay(1, 3)
    pref_copy.wait_recv()
    kv_copies += project(pref, 1 - head)
    relay(0, 4)
    relay(1, 4)
    relay(0, 5)
    relay(1, 5)
    for copy in kv_copies:
        copy.wait_recv()

    def stat_copy(step):
        return pltpu.make_async_remote_copy(
            src_ref=stat.at[step], dst_ref=stat_in.at[me],
            send_sem=stat_send.at[step], recv_sem=stat_recv.at[me],
            device_id=peer(step), device_id_type=MESH,
        )

    def glob_copy(k):
        target = lax.rem(me + k, PEERS)
        return pltpu.make_async_remote_copy(
            src_ref=glob.at[me], dst_ref=glob.at[me],
            send_sem=glob_send.at[k], recv_sem=glob_recv.at[me],
            device_id=peer(target), device_id_type=MESH,
        )

    def stat_arrival(j):
        return pltpu.make_async_remote_copy(
            src_ref=stat.at[j], dst_ref=stat_in.at[j],
            send_sem=stat_send.at[j], recv_sem=stat_recv.at[j],
            device_id=peer(j), device_id_type=MESH,
        )

    def glob_arrival(j):
        return pltpu.make_async_remote_copy(
            src_ref=glob.at[j], dst_ref=glob.at[j],
            send_sem=glob_send.at[0], recv_sem=glob_recv.at[j],
            device_id=peer(j), device_id_type=MESH,
        )

    def join():
        def arrive(k, carry):
            stat_arrival(lax.rem(me + k, PEERS)).wait_recv()
            return carry

        lax.fori_loop(1, PEERS, arrive, 0)
        stat_in[me] = stat[me]
        tops = [stat_in[j, 0:1, :] for j in range(PEERS)]
        top = tops[0]
        for j in range(1, PEERS):
            top = jnp.maximum(top, tops[j])
        total = jnp.zeros_like(top)
        inner = jnp.zeros_like(top)
        for j in range(PEERS):
            factor = jnp.exp2(tops[j] - top)
            total += stat_in[j, 1:2, :] * factor
            inner += stat_in[j, 2:3, :] * factor
        glob[me, 0:1, :] = top + jnp.log2(total)
        glob[me, 1:2, :] = inner / total

        def spread_out(k, carry):
            glob_copy(k).start()
            return carry

        lax.fori_loop(1, PEERS, spread_out, 0)

    def latent_rows(t, n, cols):
        rows = gat[t, lax.div(n, 2), pl.ds(2 * lax.rem(n, 2), 2), :, :, cols]
        return rows.reshape(TILE, HEAD_DIM)

    def forward(step, carry):
        h = lax.div(step, TILES)
        n = lax.rem(step, TILES)
        cols = lanes(h, HEAD_DIM)
        where = lanes(n, TILE)
        key = kv[0, :, :, :, cols].reshape(4 * ROWS, HEAD_DIM)
        value = kv[1, :, :, :, cols].reshape(4 * ROWS, HEAD_DIM)
        scores = dot(key, latent_rows(0, n, cols), NT)
        dots = dot(value, latent_rows(1, n, cols), NT)
        parts = []
        top = None
        for u in range(4 * ROWS // UNIT):
            row = bias[u // 6, (u // 3) % 2, u % 3 : u % 3 + 1, where]
            part = scores[u * UNIT : (u + 1) * UNIT] * SCALE2 + row
            parts.append(part)
            top = part if top is None else jnp.maximum(top, part)
        top = jnp.max(top, axis=0, keepdims=True)
        total = inner = None
        for u, part in enumerate(parts):
            weight = jnp.exp2(part - top)
            term = weight * dots[u * UNIT : (u + 1) * UNIT]
            total = weight if total is None else total + weight
            inner = term if inner is None else inner + term
        stat[step, 0:1, :] = top
        stat[step, 1:2, :] = jnp.sum(total, axis=0, keepdims=True)
        stat[step, 2:3, :] = jnp.sum(inner, axis=0, keepdims=True)

        @pl.when(step != me)
        def _():
            stat_copy(step).start()

        @pl.when(step == me + LAG)
        def _():
            join()

        return carry

    stat[...] = jnp.zeros_like(stat)
    glob[...] = jnp.zeros_like(glob)
    lax.fori_loop(0, STEPS, forward, 0)

    def backward(part, half, h):
        cols = lanes(h, HEAD_DIM)
        key = kv[0, :, half, :, cols].reshape(2 * ROWS, HEAD_DIM)
        value = kv[1, :, half, :, cols].reshape(2 * ROWS, HEAD_DIM)
        for n in range(TILES):
            step = h * TILES + n
            if part == 0:

                @pl.when(step + STEPS == me + LAG)
                def _():
                    join()

                @pl.when(step != me)
                def _():
                    glob_arrival(step).wait_recv()

            where = pl.ds(n * TILE, TILE)
            query = latent_rows(0, n, cols)
            grad = latent_rows(1, n, cols)
            scores = dot(key, query, NT)
            dots = dot(value, grad, NT)
            total = glob[step, 0:1, :]
            delta = glob[step, 1:2, :]
            for u in range(2 * ROWS // UNIT):
                rows = pl.ds(u * UNIT, UNIT)
                shift = bias[u // 3, half, u % 3 : u % 3 + 1, where] - total
                weight = jnp.exp2(scores[u * UNIT : (u + 1) * UNIT] * SCALE2 + shift)
                change = weight * (dots[u * UNIT : (u + 1) * UNIT] - delta)
                p_low[rows, where] = weight.astype(BF16)
                s_low[rows, where] = change.astype(BF16)
        query = gat[0, :, :, :, :, cols].reshape(LATENTS, HEAD_DIM)
        grad = gat[1, :, :, :, :, cols].reshape(LATENTS, HEAD_DIM)
        change = s_low[...]
        dkv[part, 0, :, :, cols] = dot(change, query, NN).reshape(2, ROWS, HEAD_DIM)
        dkv[part, 1, :, :, cols] = dot(p_low[...], grad, NN).reshape(2, ROWS, HEAD_DIM)
        query_grad = dot(change, key, TN).reshape(NZ, NX, NY, LAT, HEAD_DIM)
        if part == 0:
            dq[h] = query_grad
        else:
            dq[h] = dq[h] + query_grad
        dkv_copy(part, h).start()

    def dkv_copy(part, h):
        cols = lanes(h, HEAD_DIM)
        return pltpu.make_async_remote_copy(
            src_ref=dkv.at[part, :, 1 - core, :, cols], dst_ref=dkv_in.at[part, :, :, cols],
            send_sem=dkv_send.at[part, h], recv_sem=dkv_recv.at[part, h],
            device_id=sibling, device_id_type=MESH,
        )

    def lower(part):
        def arrive(h, carry):
            dkv_copy(part, h).wait_recv()
            return carry

        lax.fori_loop(0, HEADS, arrive, 0)
        low[0] = ((dkv[part, 0, core] + dkv_in[part, 0]) * SCALE).astype(BF16)
        low[1] = (dkv[part, 1, core] + dkv_in[part, 1]).astype(BF16)

    def back_product(j):
        rows = lanes(j, 256)
        return dot(low[0], w[0, rows, :], NT) + dot(low[1], w[1, rows, :], NT)

    def back_copy(j):
        cols = lanes(j, 256)
        return pltpu.make_async_remote_copy(
            src_ref=back.at[:, cols], dst_ref=back_in.at[:, cols],
            send_sem=back_send.at[j], recv_sem=back_recv.at[j],
            device_id=partner, device_id_type=MESH,
        )

    def first_part(h, carry):
        backward(0, 1 - head, h)
        return carry

    def second_part(h, carry):
        backward(1, head, h)
        return carry

    lax.fori_loop(0, HEADS, first_part, 0)
    lower(0)

    def back_send_out(j, carry):
        back[:, lanes(j, 256)] = back_product(j)
        back_copy(j).start()
        return carry

    lax.fori_loop(0, D // 256, back_send_out, 0)
    lax.fori_loop(0, HEADS, second_part, 0)

    size = HEADS // GROUPS
    ahead = {}

    def reduce(g, step):
        hs = pl.ds(g * size, size)
        first, second = rings[1 - g % 2]
        (p1, m1, a, a1, a3), (p2, m2, e, e1, e3) = first, second
        a2, e2 = up(a, 2), up(e, 2)

        def plane(z_, k):
            return dq.at[hs, z_, :, k] if g % 2 == 0 else dq.at[hs, z_, k]

        def planes(k):
            return dq.at[hs, :, :, k] if g % 2 == 0 else dq.at[hs, :, k]

        def cell(z_, k):
            return dq.at[hs, z_, k, a] if g % 2 == 0 else dq.at[hs, z_, a, k]

        def cells(k):
            return dq.at[hs, :, k, a] if g % 2 == 0 else dq.at[hs, :, a, k]

        def add(ref, *terms):
            value = ref[...]
            for term in terms:
                value = value + term
            ref[...] = value

        if step == 0:
            ahead[g] = [send(plane(0, a2), r1.at[g, 0], p1), send(plane(1, a2), r1.at[g, 1], m1)]
            return
        for copy in ahead[g]:
            copy.wait_recv()
        if step == 1:
            add(plane(0, a1), r1[g, 0])
            add(plane(1, a3), r1[g, 1])
            ahead[g] = [send(planes(a1), r2.at[g, 0], p1), send(planes(a3), r2.at[g, 1], m1)]
        elif step == 2:
            add(planes(a), r2[g, 0], r2[g, 1])
            ahead[g] = [send(cell(0, e2), r3.at[g, 0], p2), send(cell(1, e2), r3.at[g, 1], m2)]
        elif step == 3:
            add(cell(0, e1), r3[g, 0])
            add(cell(1, e3), r3[g, 1])
            ahead[g] = [send(cells(e1), r4.at[g, 0], p2), send(cells(e3), r4.at[g, 1], m2)]
        elif step == 4:
            add(cells(e), r4[g, 0], r4[g, 1])
            ahead[g] = [send(dq.at[hs, 1 - z, x, y], r5.at[g], zn)]
        else:
            result = ((dq[hs, z, x, y] + r5[g]) * SCALE).astype(BF16)
            for k in range(size):
                dq_out[:, pl.ds((g * size + k) * HEAD_DIM, HEAD_DIM)] = result[k]

    pairs = GROUPS // 2
    for wave in range(6 + pairs - 1):
        for g in range(GROUPS):
            if 0 <= wave - g // 2 < 6:
                reduce(g, wave - g // 2)

    lower(1)

    def finish(j, carry):
        cols = lanes(j, 256)
        mine = back_product(j)
        back_copy(j).wait_recv()
        pg_out[:, cols] = (mine + back_in[:, cols]).astype(BF16)
        return carry

    lax.fori_loop(0, D // 256, finish, 0)

    for copy in used:
        copy.wait_send()

    def settle(k, carry):
        stat_copy(lax.rem(me + k, PEERS)).wait_send()
        glob_copy(k).wait_send()
        return carry

    lax.fori_loop(1, PEERS, settle, 0)

    def settle_heads(h, carry):
        dkv_copy(0, h).wait_send()
        dkv_copy(1, h).wait_send()
        back_copy(h).wait_send()
        return carry

    lax.fori_loop(0, HEADS, settle_heads, 0)


def local(prefix, w_key, w_value, queries, output_grad, block_mask):
    live = (block_mask != 0).astype(F32).reshape(PEERS, 2, 3).transpose(1, 2, 0)
    units = jnp.repeat(live, BLOCK // UNIT, axis=1).reshape(2, 2, 3, PEERS)
    mask = jnp.pad(units, ((0, 0), (0, 0), (0, 5), (0, BLOCK - PEERS)))
    size = HEADS // GROUPS
    vmem = pl.BlockSpec(memory_space=pltpu.VMEM)
    hbm = pl.BlockSpec(memory_space=pl.ANY)
    dma = pltpu.SemaphoreType.DMA
    copies = 2 * CHUNKS * 13 + 1 + 1 + 4 + GROUPS * 9
    return pl.pallas_call(
        kernel,
        out_shape=(
            jax.ShapeDtypeStruct((LAT, COLS), BF16),
            jax.ShapeDtypeStruct((ROWS, D), BF16),
        ),
        in_specs=[vmem, hbm, hbm, vmem, vmem, vmem],
        out_specs=(vmem, vmem),
        scratch_shapes=[
            pltpu.VMEM((2, D, COLS), BF16),
            pltpu.VMEM((ROWS, D), BF16),
            pltpu.VMEM((2, NZ, NX, NY, LAT, COLS), BF16),
            pltpu.VMEM((2, 2, 2, ROWS, COLS), BF16),
            pltpu.VMEM((2, 8, BLOCK), F32),
            pltpu.VMEM((2, 2, 8, LATENTS), F32),
            pltpu.VMEM((STEPS, 8, TILE), F32),
            pltpu.VMEM((PEERS, 8, TILE), F32),
            pltpu.VMEM((STEPS, 8, TILE), F32),
            pltpu.VMEM((2 * ROWS, LATENTS), BF16),
            pltpu.VMEM((2 * ROWS, LATENTS), BF16),
            pltpu.VMEM((HEADS, NZ, NX, NY, LAT, HEAD_DIM), F32),
            pltpu.VMEM((GROUPS, 2, size, 4, LAT, HEAD_DIM), F32),
            pltpu.VMEM((GROUPS, 2, size, NZ, 4, LAT, HEAD_DIM), F32),
            pltpu.VMEM((GROUPS, 2, size, LAT, HEAD_DIM), F32),
            pltpu.VMEM((GROUPS, 2, size, NZ, LAT, HEAD_DIM), F32),
            pltpu.VMEM((GROUPS, size, LAT, HEAD_DIM), F32),
            pltpu.VMEM((2, 2, 2, ROWS, COLS), F32),
            pltpu.VMEM((2, 2, ROWS, COLS), F32),
            pltpu.VMEM((2, ROWS, COLS), BF16),
            pltpu.VMEM((ROWS, D), F32),
            pltpu.VMEM((ROWS, D), F32),
            dma((2,)),
            dma((2 * CHUNKS,)),
            dma((copies,)),
            dma((copies,)),
            dma((STEPS,)),
            dma((PEERS,)),
            dma((PEERS,)),
            dma((PEERS,)),
            dma((2, HEADS)),
            dma((2, HEADS)),
            dma((D // 256,)),
            dma((D // 256,)),
        ],
        compiler_params=pltpu.CompilerParams(
            collective_id=0, has_side_effects=True, vmem_limit_bytes=60 << 20
        ),
        cost_estimate=pl.CostEstimate(
            flops=20_000_000_000, bytes_accessed=12 << 20, transcendentals=13_000_000
        ),
        name="attention_backward",
    )(prefix, w_key, w_value, queries, output_grad, mask)


def solution(mesh):
    return jax.shard_map(
        local,
        mesh=mesh,
        in_specs=(
            P(("blk", "head"), None),
            P(None, "head"),
            P(None, "head"),
            P("blk", "head"),
            P("blk", "head"),
            P(None, "blk"),
        ),
        out_specs=(P("blk", "head"), P(("blk", "head"), None)),
        check_vma=False,
    )
```

```python
import math

import jax
import jax.numpy as jnp
from jax import lax
from jax.experimental import pallas as pl
from jax.experimental.pallas import tpu as pltpu
from jax.sharding import PartitionSpec as P

MESH = pl.DeviceIdType.MESH
HEAD_DIM = 128
BLOCK = 128
UNIT = 64
FILL = -1e30
F32 = jnp.float32
BF16 = jnp.bfloat16

NZ, NX, NY = 2, 4, 4
PEERS = NZ * NX * NY
HEADS = 8
LAT = 32
ROWS = 192
COLS = HEADS * HEAD_DIM
D = 2048
LATENTS = PEERS * LAT
TILE = 256
TILES = LATENTS // TILE
STEPS = HEADS * TILES
LAG = 16
CHUNKS = 2
PAD = 16
SCALE = 1.0 / math.sqrt(HEAD_DIM)
SCALE2 = SCALE * math.log2(math.e)
NT = (((1,), (1,)), ((), ()))
TN = (((0,), (0,)), ((), ()))
NN = (((1,), (0,)), ((), ()))


def dot(a, b, dims):
    return lax.dot_general(a, b, dims, preferred_element_type=F32)


def encode(value):
    top = jnp.max(jnp.abs(value), axis=0, keepdims=True)
    power = jnp.floor(jnp.log2(top + 1e-30) * 64.0) + 2.0
    whole = jnp.round(value * (jnp.exp2(power * (-1.0 / 64.0)) * 32767.0))
    powers = jnp.broadcast_to(power, (PAD, value.shape[1]))
    return whole.astype(jnp.int32).astype(jnp.int16), powers.astype(jnp.int32).astype(jnp.int16)


def put(ref, value):
    rows = value.shape[0]
    ref[0:rows], ref[rows : rows + PAD] = encode(value)


def decode(ref, rows):
    power = ref[rows : rows + PAD].astype(jnp.int32).astype(F32)[0:1]
    return ref[0:rows].astype(jnp.int32).astype(F32) * (
        jnp.exp2(power * (1.0 / 64.0)) * (1.0 / 32767.0)
    )


def lanes(index, width):
    return pl.ds(pl.multiple_of(index * width, width), width)


def kernel(
    prefix, w_key, w_value, queries, grads, mask,
    dq_out, pg_out,
    w, pref, gat, kv, mask_in, bias, stat, stat_in, glob, p_low, s_low, dq,
    e1, e2, e3, e4, e5, r1, r2, r3, r4, r5, dkv, dkv_in, low, back, back_out, back_in,
    w_sem, own_sem, send_sem, recv_sem, stat_send, stat_recv, glob_send, glob_recv,
    dkv_send, dkv_recv, back_send, back_recv,
):
    b = lax.axis_index("blk")
    head = lax.axis_index("head")
    core = lax.rem(b, 2)
    me = lax.div(b, 2)
    y = lax.rem(me, NY)
    x = lax.rem(lax.div(me, NY), NX)
    z = lax.div(me, NX * NY)

    def peer(index):
        return (2 * index + core, head)

    def at(z_, x_, y_):
        return peer((z_ * NX + x_) * NY + y_)

    up = lambda v, k: lax.rem(v + k, 4)
    x1, x2, x3 = up(x, 1), up(x, 2), up(x, 3)
    y1, y2, y3 = up(y, 1), up(y, 2), up(y, 3)
    xp, xm, yp, ym, zn = at(z, x1, y), at(z, x3, y), at(z, x, y1), at(z, x, y3), at(1 - z, x, y)
    sibling = (2 * me + 1 - core, head)
    partner = (b, 1 - head)

    barrier = pltpu.get_barrier_semaphore()

    def greet(k, carry):
        pl.semaphore_signal(
            barrier, inc=1, device_id=peer(lax.rem(me + k, PEERS)), device_id_type=MESH
        )
        return carry

    lax.fori_loop(1, PEERS, greet, 0)
    pl.semaphore_signal(barrier, inc=1, device_id=sibling, device_id_type=MESH)
    pl.semaphore_signal(barrier, inc=1, device_id=partner, device_id_type=MESH)

    w_copies = [
        pltpu.make_async_copy(w_key, w.at[0], w_sem.at[0]),
        pltpu.make_async_copy(w_value, w.at[1], w_sem.at[1]),
    ]
    for copy in w_copies:
        copy.start()
    pl.semaphore_wait(barrier, PEERS + 1)

    used = []

    def send(src, dst, device):
        index = len(used)

        def view(place):
            return place[0].at[place[1:]] if isinstance(place, tuple) else place

        def copy():
            return pltpu.make_async_remote_copy(
                src_ref=view(src), dst_ref=view(dst),
                send_sem=send_sem.at[index], recv_sem=recv_sem.at[index],
                device_id=device, device_id_type=MESH,
            )

        copy().start()
        used.append(copy)
        return copy

    shards = (queries, grads)
    along_x, along_y = (xp, xm, x, x1, x2, x3), (yp, ym, y, y1, y2, y3)
    rings = ((along_x, along_y), (along_y, along_x))

    def block(t, z_, first, second, cols):
        if t == 0:
            return gat.at[0, z_, first, second, :, cols]
        return gat.at[1, z_, second, first, :, cols]

    def line(t, z_, second, cols):
        if t == 0:
            return gat.at[0, z_, :, second, :, cols]
        return gat.at[1, z_, second, :, :, cols]

    width = COLS // CHUNKS
    flight = {}

    def relay(c, step):
        cols = pl.ds(c * width, width)
        for t in range(2):
            (p1, m1, a, a_up, _, a_dn), (p2, m2, e, e_up, _, e_dn) = rings[t]
            key = (c, t)
            if step == 0:
                mine = shards[t].at[:, cols]
                dst = block(t, z, a, e, cols)
                own = pltpu.make_async_copy(mine, dst, own_sem.at[2 * c + t])
                own.start()
                flight[key] = [send(mine, dst, zn), send(mine, dst, p1), send(mine, dst, m1), own]
            elif step == 1:
                flight[key][0]().wait_recv()
                src = block(t, 1 - z, a, e, cols)
                flight[key] += [send(src, src, p1), send(src, src, m1)]
            elif step == 2:
                for k in (1, 2, 4, 5):
                    flight[key][k]().wait_recv()
                flight[key][3].wait()
                lo, hi = block(t, 0, a_dn, e, cols), block(t, 1, a_up, e, cols)
                flight[key] = [send(lo, lo, p1), send(hi, hi, m1)]
            elif step == 3:
                for k in (0, 1):
                    flight[key][k]().wait_recv()
                flight[key] = []
                for z_ in range(NZ):
                    src = line(t, z_, e, cols)
                    flight[key] += [send(src, src, p2), send(src, src, m2)]
            elif step == 4:
                for k in range(4):
                    flight[key][k]().wait_recv()
                lo, hi = line(t, 0, e_dn, cols), line(t, 1, e_up, cols)
                flight[key] = [send(lo, lo, p2), send(hi, hi, m2)]
            else:
                for k in (0, 1):
                    flight[key][k]().wait_recv()

    for c in range(CHUNKS):
        relay(c, 0)
    pref_copy = send(prefix, pref, partner)
    mask_copy = send(mask, mask_in, sibling)

    def project(rows, half):
        def column(j, carry):
            for i in range(2):
                cols = lanes(j, 256)
                kv[i, core, half, :, cols] = dot(rows[...], w[i, :, cols], NN).astype(BF16)
            return carry

        lax.fori_loop(0, COLS // 256, column, 0)
        return [send(kv.at[i, core, half], kv.at[i, core, half], sibling) for i in range(2)]

    relay(0, 1)
    relay(1, 1)
    for copy in w_copies:
        copy.wait()
    kv_copies = project(prefix, head)
    relay(0, 2)
    relay(1, 2)

    group = lax.broadcasted_iota(jnp.int32, (2 * PEERS, LATENTS), 0)
    latent = lax.broadcasted_iota(jnp.int32, (2 * PEERS, LATENTS), 1)
    spread = jnp.where(2 * lax.div(latent, LAT) + core == group, 1.0, 0.0).astype(BF16)

    def fill_bias(row_core, source):
        live = dot(jnp.where(source[...] != 0, 1.0, 0.0).astype(BF16), spread, TN)
        for unit in range(2 * ROWS // UNIT):
            row = live[unit * UNIT // BLOCK : unit * UNIT // BLOCK + 1]
            bias[row_core, unit // 3, unit % 3 : unit % 3 + 1, :] = jnp.where(row > 0.5, 0.0, FILL)

    fill_bias(core, mask)
    mask_copy().wait_recv()
    fill_bias(1 - core, mask_in)
    relay(0, 3)
    relay(1, 3)
    pref_copy().wait_recv()
    kv_copies += project(pref, 1 - head)
    relay(0, 4)
    relay(1, 4)
    relay(0, 5)
    relay(1, 5)
    for copy in kv_copies:
        copy().wait_recv()

    def stat_copy(step):
        return pltpu.make_async_remote_copy(
            src_ref=stat.at[step], dst_ref=stat_in.at[me],
            send_sem=stat_send.at[step], recv_sem=stat_recv.at[me],
            device_id=peer(step), device_id_type=MESH,
        )

    def glob_copy(k):
        target = lax.rem(me + k, PEERS)
        return pltpu.make_async_remote_copy(
            src_ref=glob.at[me], dst_ref=glob.at[me],
            send_sem=glob_send.at[k], recv_sem=glob_recv.at[me],
            device_id=peer(target), device_id_type=MESH,
        )

    def stat_arrival(j):
        return pltpu.make_async_remote_copy(
            src_ref=stat.at[j], dst_ref=stat_in.at[j],
            send_sem=stat_send.at[j], recv_sem=stat_recv.at[j],
            device_id=peer(j), device_id_type=MESH,
        )

    def glob_arrival(j):
        return pltpu.make_async_remote_copy(
            src_ref=glob.at[j], dst_ref=glob.at[j],
            send_sem=glob_send.at[0], recv_sem=glob_recv.at[j],
            device_id=peer(j), device_id_type=MESH,
        )

    def join():
        def arrive(k, carry):
            stat_arrival(lax.rem(me + k, PEERS)).wait_recv()
            return carry

        lax.fori_loop(1, PEERS, arrive, 0)
        stat_in[me] = stat[me]
        tops = [stat_in[j, 0:1, :] for j in range(PEERS)]
        top = tops[0]
        for j in range(1, PEERS):
            top = jnp.maximum(top, tops[j])
        total = jnp.zeros_like(top)
        inner = jnp.zeros_like(top)
        for j in range(PEERS):
            factor = jnp.exp2(tops[j] - top)
            total += stat_in[j, 1:2, :] * factor
            inner += stat_in[j, 2:3, :] * factor
        glob[me, 0:1, :] = top + jnp.log2(total)
        glob[me, 1:2, :] = inner / total

        def spread_out(k, carry):
            glob_copy(k).start()
            return carry

        lax.fori_loop(1, PEERS, spread_out, 0)

    def latent_rows(t, n, cols):
        rows = gat[t, lax.div(n, 2), pl.ds(2 * lax.rem(n, 2), 2), :, :, cols]
        return rows.reshape(TILE, HEAD_DIM)

    def forward(step, carry):
        h = lax.div(step, TILES)
        n = lax.rem(step, TILES)
        cols = lanes(h, HEAD_DIM)
        where = lanes(n, TILE)
        key = kv[0, :, :, :, cols].reshape(4 * ROWS, HEAD_DIM)
        value = kv[1, :, :, :, cols].reshape(4 * ROWS, HEAD_DIM)
        scores = dot(key, latent_rows(0, n, cols), NT)
        dots = dot(value, latent_rows(1, n, cols), NT)
        parts = []
        top = None
        for u in range(4 * ROWS // UNIT):
            row = bias[u // 6, (u // 3) % 2, u % 3 : u % 3 + 1, where]
            part = scores[u * UNIT : (u + 1) * UNIT] * SCALE2 + row
            parts.append(part)
            top = part if top is None else jnp.maximum(top, part)
        top = jnp.max(top, axis=0, keepdims=True)
        total = inner = None
        for u, part in enumerate(parts):
            weight = jnp.exp2(part - top)
            term = weight * dots[u * UNIT : (u + 1) * UNIT]
            total = weight if total is None else total + weight
            inner = term if inner is None else inner + term
        stat[step, 0:1, :] = top
        stat[step, 1:2, :] = jnp.sum(total, axis=0, keepdims=True)
        stat[step, 2:3, :] = jnp.sum(inner, axis=0, keepdims=True)

        @pl.when(step != me)
        def _():
            stat_copy(step).start()

        @pl.when(step == me + LAG)
        def _():
            join()

        return carry

    stat[...] = jnp.zeros_like(stat)
    glob[...] = jnp.zeros_like(glob)
    lax.fori_loop(0, STEPS, forward, 0)

    def backward(part, half, h):
        cols = lanes(h, HEAD_DIM)
        key = kv[0, :, half, :, cols].reshape(2 * ROWS, HEAD_DIM)
        value = kv[1, :, half, :, cols].reshape(2 * ROWS, HEAD_DIM)
        for n in range(TILES):
            step = h * TILES + n
            if part == 0:

                @pl.when(step + STEPS == me + LAG)
                def _():
                    join()

                @pl.when(step != me)
                def _():
                    glob_arrival(step).wait_recv()

            where = pl.ds(n * TILE, TILE)
            query = latent_rows(0, n, cols)
            grad = latent_rows(1, n, cols)
            scores = dot(key, query, NT)
            dots = dot(value, grad, NT)
            total = glob[step, 0:1, :]
            delta = glob[step, 1:2, :]
            for u in range(2 * ROWS // UNIT):
                rows = pl.ds(u * UNIT, UNIT)
                shift = bias[u // 3, half, u % 3 : u % 3 + 1, where] - total
                weight = jnp.exp2(scores[u * UNIT : (u + 1) * UNIT] * SCALE2 + shift)
                change = weight * (dots[u * UNIT : (u + 1) * UNIT] - delta)
                p_low[rows, where] = weight.astype(BF16)
                s_low[rows, where] = change.astype(BF16)
        query = gat[0, :, :, :, :, cols].reshape(LATENTS, HEAD_DIM)
        grad = gat[1, :, :, :, :, cols].reshape(LATENTS, HEAD_DIM)
        change = s_low[...]
        dkv[part, 0, :, :, cols] = dot(change, query, NN).reshape(2, ROWS, HEAD_DIM)
        dkv[part, 1, :, :, cols] = dot(p_low[...], grad, NN).reshape(2, ROWS, HEAD_DIM)
        query_grad = dot(change, key, TN).reshape(NZ, NX, NY, LAT, HEAD_DIM)
        if part == 0:
            dq[h] = query_grad
        else:
            dq[h] = dq[h] + query_grad
        dkv_copy(part, h).start()

    def dkv_copy(part, h):
        cols = lanes(h, HEAD_DIM)
        return pltpu.make_async_remote_copy(
            src_ref=dkv.at[part, :, 1 - core, :, cols], dst_ref=dkv_in.at[part, :, :, cols],
            send_sem=dkv_send.at[part, h], recv_sem=dkv_recv.at[part, h],
            device_id=sibling, device_id_type=MESH,
        )

    def lower(part):
        def arrive(h, carry):
            dkv_copy(part, h).wait_recv()
            return carry

        lax.fori_loop(0, HEADS, arrive, 0)
        low[0] = ((dkv[part, 0, core] + dkv_in[part, 0]) * SCALE).astype(BF16)
        low[1] = (dkv[part, 1, core] + dkv_in[part, 1]).astype(BF16)

    def back_product(j):
        rows = lanes(j, 256)
        return dot(low[0], w[0, rows, :], NT) + dot(low[1], w[1, rows, :], NT)

    def back_copy(j):
        return pltpu.make_async_remote_copy(
            src_ref=back_out.at[j], dst_ref=back_in.at[j],
            send_sem=back_send.at[j], recv_sem=back_recv.at[j],
            device_id=partner, device_id_type=MESH,
        )

    def first_part(h, carry):
        backward(0, 1 - head, h)
        return carry

    lax.fori_loop(0, HEADS, first_part, 0)
    lower(0)

    def back_send_out(j, carry):
        put(back_out.at[j], back_product(j))
        back_copy(j).start()
        return carry

    lax.fori_loop(0, D // 256, back_send_out, 0)

    ahead = {}
    cell_rows = LAT
    line_rows = 4 * LAT

    def reduce(h, step):
        (p1, m1, a, a1, a2, a3), (p2, m2, f, f1, f2, f3) = rings[1 - h % 2]

        def line_ref(z_, k):
            return dq.at[h, z_, :, k] if h % 2 == 0 else dq.at[h, z_, k]

        def line_of(z_, k):
            return line_ref(z_, k)[...].reshape(line_rows, HEAD_DIM)

        def cell_ref(z_, k):
            return dq.at[h, z_, k, a] if h % 2 == 0 else dq.at[h, z_, a, k]

        for copy in ahead.get(h, ()):
            copy().wait_recv()
        if step == 0:
            put(e1.at[h, 0], line_of(0, a2))
            put(e1.at[h, 1], line_of(1, a2))
            ahead[h] = [send((e1, h, 0), (r1, h, 0), p1), send((e1, h, 1), (r1, h, 1), m1)]
        elif step == 1:
            put(e2.at[h, 0, 0], line_of(0, a1) + decode(r1.at[h, 0], line_rows))
            put(e2.at[h, 0, 1], line_of(1, a1))
            put(e2.at[h, 1, 0], line_of(0, a3))
            put(e2.at[h, 1, 1], line_of(1, a3) + decode(r1.at[h, 1], line_rows))
            ahead[h] = [send((e2, h, 0), (r2, h, 0), p1), send((e2, h, 1), (r2, h, 1), m1)]
        elif step == 2:
            for z_ in range(NZ):
                total = line_of(z_, a)
                for k in range(2):
                    total += decode(r2.at[h, k, z_], line_rows)
                line_ref(z_, a)[...] = total.reshape(4, LAT, HEAD_DIM)
            put(e3.at[h, 0], cell_ref(0, f2)[...])
            put(e3.at[h, 1], cell_ref(1, f2)[...])
            ahead[h] = [send((e3, h, 0), (r3, h, 0), p2), send((e3, h, 1), (r3, h, 1), m2)]
        elif step == 3:
            put(e4.at[h, 0, 0], cell_ref(0, f1)[...] + decode(r3.at[h, 0], cell_rows))
            put(e4.at[h, 0, 1], cell_ref(1, f1)[...])
            put(e4.at[h, 1, 0], cell_ref(0, f3)[...])
            put(e4.at[h, 1, 1], cell_ref(1, f3)[...] + decode(r3.at[h, 1], cell_rows))
            ahead[h] = [send((e4, h, 0), (r4, h, 0), p2), send((e4, h, 1), (r4, h, 1), m2)]
        elif step == 4:
            for z_ in range(NZ):
                total = cell_ref(z_, f)[...]
                for k in range(2):
                    total += decode(r4.at[h, k, z_], cell_rows)
                cell_ref(z_, f)[...] = total
            put(e5.at[h], cell_ref(1 - z, f)[...])
            ahead[h] = [send((e5, h), (r5, h), zn)]
        else:
            result = cell_ref(z, f)[...] + decode(r5.at[h], cell_rows)
            dq_out[:, h * HEAD_DIM : (h + 1) * HEAD_DIM] = (result * SCALE).astype(BF16)

    pairs = HEADS // 2

    def wave(index):
        for p in range(pairs):
            if 0 <= index - p < 6:
                reduce(2 * p, index - p)
                reduce(2 * p + 1, index - p)

    def second_waves(h, carry):
        backward(1, head, h)
        for p in range(pairs):

            @pl.when(h == 2 * p + 1)
            def _():
                wave(p)

        return carry

    lax.fori_loop(0, HEADS, second_waves, 0)

    def own_product(j, carry):
        back[:, lanes(j, 256)] = back_product(j)
        return carry

    wave(pairs)
    lower(1)
    lax.fori_loop(0, D // 256, own_product, 0)
    for index in range(pairs + 1, pairs + 5):
        wave(index)

    def finish(j, carry):
        cols = lanes(j, 256)
        back_copy(j).wait_recv()
        pg_out[:, cols] = (back[:, cols] + decode(back_in.at[j], ROWS)).astype(BF16)
        return carry

    lax.fori_loop(0, D // 256, finish, 0)

    for copy in used:
        copy().wait_send()

    def settle(k, carry):
        stat_copy(lax.rem(me + k, PEERS)).wait_send()
        glob_copy(k).wait_send()
        return carry

    lax.fori_loop(1, PEERS, settle, 0)

    def settle_heads(h, carry):
        dkv_copy(0, h).wait_send()
        dkv_copy(1, h).wait_send()
        back_copy(h).wait_send()
        return carry

    lax.fori_loop(0, HEADS, settle_heads, 0)


def local(prefix, w_key, w_value, queries, output_grad, block_mask):
    vmem = pl.BlockSpec(memory_space=pltpu.VMEM)
    hbm = pl.BlockSpec(memory_space=pl.ANY)
    dma = pltpu.SemaphoreType.DMA
    copies = 2 * CHUNKS * 13 + 1 + 1 + 4 + HEADS * 9
    line, cell = 4 * LAT + PAD, LAT + PAD
    coded = [
        pltpu.VMEM((HEADS, 2, line, HEAD_DIM), jnp.int16),
        pltpu.VMEM((HEADS, 2, NZ, line, HEAD_DIM), jnp.int16),
        pltpu.VMEM((HEADS, 2, cell, HEAD_DIM), jnp.int16),
        pltpu.VMEM((HEADS, 2, NZ, cell, HEAD_DIM), jnp.int16),
        pltpu.VMEM((HEADS, cell, HEAD_DIM), jnp.int16),
    ]
    return pl.pallas_call(
        kernel,
        out_shape=(
            jax.ShapeDtypeStruct((LAT, COLS), BF16),
            jax.ShapeDtypeStruct((ROWS, D), BF16),
        ),
        in_specs=[vmem, hbm, hbm, vmem, vmem, vmem],
        out_specs=(vmem, vmem),
        scratch_shapes=[
            pltpu.VMEM((2, D, COLS), BF16),
            pltpu.VMEM((ROWS, D), BF16),
            pltpu.VMEM((2, NZ, NX, NY, LAT, COLS), BF16),
            pltpu.VMEM((2, 2, 2, ROWS, COLS), BF16),
            pltpu.VMEM((2 * PEERS, 3), jnp.int32),
            pltpu.VMEM((2, 2, 8, LATENTS), F32),
            pltpu.VMEM((STEPS, 8, TILE), F32),
            pltpu.VMEM((PEERS, 8, TILE), F32),
            pltpu.VMEM((STEPS, 8, TILE), F32),
            pltpu.VMEM((2 * ROWS, LATENTS), BF16),
            pltpu.VMEM((2 * ROWS, LATENTS), BF16),
            pltpu.VMEM((HEADS, NZ, NX, NY, LAT, HEAD_DIM), F32),
            *coded,
            *coded,
            pltpu.VMEM((2, 2, 2, ROWS, COLS), F32),
            pltpu.VMEM((2, 2, ROWS, COLS), F32),
            pltpu.VMEM((2, ROWS, COLS), BF16),
            pltpu.VMEM((ROWS, D), F32),
            pltpu.VMEM((D // 256, ROWS + PAD, 256), jnp.int16),
            pltpu.VMEM((D // 256, ROWS + PAD, 256), jnp.int16),
            dma((2,)),
            dma((2 * CHUNKS,)),
            dma((copies,)),
            dma((copies,)),
            dma((STEPS,)),
            dma((PEERS,)),
            dma((PEERS,)),
            dma((PEERS,)),
            dma((2, HEADS)),
            dma((2, HEADS)),
            dma((D // 256,)),
            dma((D // 256,)),
        ],
        compiler_params=pltpu.CompilerParams(
            collective_id=0, has_side_effects=True, vmem_limit_bytes=60 << 20
        ),
        cost_estimate=pl.CostEstimate(
            flops=20_000_000_000, bytes_accessed=12 << 20, transcendentals=13_000_000
        ),
        name="attention_backward",
    )(prefix, w_key, w_value, queries, output_grad, block_mask)


def solution(mesh):
    return jax.shard_map(
        local,
        mesh=mesh,
        in_specs=(
            P(("blk", "head"), None),
            P(None, "head"),
            P(None, "head"),
            P("blk", "head"),
            P("blk", "head"),
            P(None, "blk"),
        ),
        out_specs=(P("blk", "head"), P(("blk", "head"), None)),
        check_vma=False,
    )
```
